512 devices in a mesh: dp: 2 (over core), ctx: 32 (over z, y_hi), tp: 8 (over x, y_lo).
Axes of the slice: x: 4, y: 8 (y_hi: 4, y_lo: 2; y = y_hi * 2 + y_lo), z: 8, core: 2. Of those that a mesh axis runs over, the one named last changes fastest.
Arguments:
- tokens: bfloat16 [32768, 4096], P(('dp', 'ctx')), parts along dimension 0, may hold values from -6 to 6
- lengths: int32 [128], P('dp'), parts along dimension 0, may hold values from 1 to 1537, 16384 in all
- q_weight: bfloat16 [4096, 8, 512], P('ctx', 'tp'), may hold values from -1 to 1
- kv_weight: bfloat16 [4096, 8, 256], P('ctx', 'tp'), may hold values from -1 to 1
Outputs:
- context: bfloat16 [32768, 8, 512], P(('dp', 'ctx'), 'tp'), parts along dimension 0
The draws below stay inside these ranges and needn't reach their ends.
There are 2 independent parts, one for each index of `dp`. The reference program is written for one: setup_inputs(seed, part) draws one part's arguments, and reference() takes and returns one part's arrays. A program takes and returns all parts, laid end to end along the dimension named above; an argument that names none is the same for every part. Nothing has to cross between parts.
Inputs may be any that keep to these rules, and one draw needn't show every extreme that they name: The lengths sum to 16384 and the longest is exactly 1537.
All inputs are finite; a program needn't handle non-finite values.
Results may differ from the reference program's by a relative error of at most 0.0064.
Values may be sent and summed in bfloat16 or wider, within the bound.
No kernel may reach another device: no remote copies, remote signals or barrier semaphores. Data moves between devices by JAX's collectives and lax.ppermute only.
A program may use at most 128 MiB of HBM per device.

```python
import math
import jax
import jax.numpy as jnp
import numpy as np
from jax import lax

D = 4096
HD = 128
QH_DEV = 4
TOK_DEV = 512
DOCS = 64
TOKENS = 16384
GROUPS = 8
LONGEST = 1537
N_CTX = 32


def clipped_normal(key, shape):
    return jnp.clip(jax.random.normal(key, shape, jnp.float32), -4.0, 4.0)


def draw_q_weight(key, part):
    noise_key = jax.random.fold_in(key, 1)
    noise_part = clipped_normal(noise_key, (D, GROUPS, QH_DEV * HD))
    combined = noise_part
    return (combined / math.sqrt(D)).astype(jnp.bfloat16)


def draw_kv_weight(key, part):
    noise_key = jax.random.fold_in(key, 2)
    noise_part = clipped_normal(noise_key, (D, GROUPS, 2 * HD))
    combined = noise_part
    return (combined / math.sqrt(D)).astype(jnp.bfloat16)


def draw_tokens(key, part):
    key = jax.random.fold_in(key, 3)
    combined = jnp.clip(jax.random.normal(key, (TOKENS, D), jnp.float32), -6.0, 6.0)
    return combined.astype(jnp.bfloat16)


def split_up(count, total, reach, slope):
    portions = [(1 << 20) // math.isqrt(standing ** slope) + 1 for standing in range(2, count + 1)]
    surplus, given = total - reach - (count - 1), [1] * (count - 1)
    while surplus > 0:
        candidates = [i for i in range(count - 1) if given[i] < reach]
        mass, left = sum([portions[i] for i in candidates]), surplus
        for i in candidates:
            more = min(reach - given[i], max(1, left * portions[i] // mass), surplus)
            given[i] = given[i] + more
            surplus = surplus - more
    return np.array([reach] + given)


def ragged(key, number_of, total, limit, lean):
    if number_of == 2:
        one = jax.random.randint(key, (), max(1, total - limit), min(limit, total - 1) + 1)
        return jnp.stack([one, total - one])
    tallies = jnp.asarray(split_up(number_of, total, limit, lean), jnp.int32)
    couples = (number_of - 1) // 2
    giver, receiver = tallies[1:1 + 2 * couples:2], tallies[2:2 + 2 * couples:2]
    slack = jnp.minimum(giver - 1, limit - receiver)
    passed = jax.random.randint(jax.random.fold_in(key, 1), (couples,), 0, 1 << 20) % (slack + 1)
    tallies = tallies.at[1:1 + 2 * couples:2].set(giver - passed).at[2:2 + 2 * couples:2].set(receiver + passed)
    return tallies[jax.random.permutation(jax.random.fold_in(key, 2), number_of)]


def setup_inputs(seed: int = 0, part: int = 0) -> dict:
    arg_keys = jax.random.split(jax.random.key(seed), 5)
    part_keys = jax.random.split(jax.random.fold_in(arg_keys[4], part), 5)
    return {
        "tokens": draw_tokens(jax.random.fold_in(jax.random.fold_in(arg_keys[4], part), 71), part),
        "lengths": ragged(part_keys[1], DOCS, TOKENS, LONGEST, 2).astype(jnp.int32),
        "q_weight": draw_q_weight(jax.random.fold_in(arg_keys[4], 71), part),
        "kv_weight": draw_kv_weight(jax.random.fold_in(arg_keys[4], 71), part),
    }


masked_score = -1e+30

def rotate(values, positions):
    half = values.shape[-1] // 2
    freqs = jnp.exp(jnp.arange(half, dtype=jnp.float32) * (-2.0 * math.log(500000.0) / values.shape[-1]))
    angle = positions.astype(jnp.float32)[:, None] * freqs[None, :]
    cosine = jnp.cos(angle)[:, None, None, :]
    sine = jnp.sin(angle)[:, None, None, :]
    first = values[..., :half]
    second = values[..., half:]
    return jnp.concatenate([first * cosine - second * sine, second * cosine + first * sine], axis=-1)

def document_of(positions, doc_ends):
    return lax.optimization_barrier(jnp.sum((positions[:, None] >= doc_ends[None, :]).astype(jnp.int32), axis=1))

def attend(queries, keys, values, query_pos, key_pos, doc_ends):
    visible = (key_pos[None, :] >= 0) & (key_pos[None, :] <= query_pos[:, None])
    visible = visible & (document_of(query_pos, doc_ends)[:, None] == document_of(key_pos, doc_ends)[None, :])
    scores = jnp.einsum('tghd,kgd->ghtk', queries.astype(jnp.float32), keys.astype(jnp.float32))
    scores = scores / math.sqrt(queries.shape[-1])
    scores = jnp.where(visible[None, None], scores, masked_score)
    peak = lax.optimization_barrier(jnp.max(scores, axis=-1, keepdims=True))
    weights = jnp.exp(scores - peak)
    probs = (weights / lax.optimization_barrier(jnp.sum(weights, axis=-1, keepdims=True))).astype(jnp.bfloat16)
    result = jnp.einsum('ghtk,kgd->tghd', probs.astype(jnp.float32), values.astype(jnp.float32))
    return result.reshape(result.shape[0], result.shape[1], -1).astype(jnp.bfloat16)

def reference(tokens, lengths, q_weight, kv_weight):
    total = tokens.shape[0]
    groups = q_weight.shape[1]
    doc_ends = jnp.cumsum(lengths).astype(jnp.int32)
    positions = jnp.arange(total, dtype=jnp.int32)
    q_raw = jnp.dot(tokens, q_weight.reshape(D, -1), preferred_element_type=jnp.float32)
    q_raw = q_raw.reshape(total, groups, QH_DEV, HD)
    kv_raw = jnp.dot(tokens, kv_weight.reshape(D, -1), preferred_element_type=jnp.float32)
    kv_raw = kv_raw.reshape(total, groups, 2 * HD)
    queries = rotate(q_raw, positions).astype(jnp.bfloat16)
    keys = rotate(kv_raw[:, :, None, :HD], positions)[:, :, 0, :].astype(jnp.bfloat16)
    values = kv_raw[:, :, HD:].astype(jnp.bfloat16)
    padding = jnp.zeros((3 * TOK_DEV, groups, HD), jnp.bfloat16)
    keys_padded = jnp.concatenate([padding, keys], axis=0)
    values_padded = jnp.concatenate([padding, values], axis=0)

    def one_block(block):
        start = (block * TOK_DEV).astype(jnp.int32)
        q_block = lax.dynamic_slice_in_dim(queries, start, TOK_DEV, 0)
        k_block = lax.dynamic_slice_in_dim(keys_padded, start, 4 * TOK_DEV, 0)
        v_block = lax.dynamic_slice_in_dim(values_padded, start, 4 * TOK_DEV, 0)
        query_pos = start + jnp.arange(TOK_DEV, dtype=jnp.int32)
        key_pos = start - 3 * TOK_DEV + jnp.arange(4 * TOK_DEV, dtype=jnp.int32)
        return attend(q_block, k_block, v_block, query_pos, key_pos, doc_ends)
    blocks = lax.map(one_block, jnp.arange(N_CTX, dtype=jnp.int32))
    return blocks.reshape(total, groups, QH_DEV * HD)
```

```python
import functools
import math

import jax
import jax.numpy as jnp
from jax import lax
from jax.experimental import pallas as pl
from jax.experimental.pallas import tpu as pltpu
from jax.sharding import Mesh
from jax.sharding import PartitionSpec as P

masked_score = -1e30
axes = ("dp", "z", "yh", "x", "yl")
z_size, yh_size, x_size, yl_size = (8, 4, 4, 2)
vmem_bytes = 48 * 1024 * 1024
tile = 128


def flat_device(dp, shard, column):
    return (dp * z_size * yh_size + shard) * (x_size * yl_size) + column


def shift_pairs(step):
    count = z_size * yh_size
    return [
        (flat_device(dp, shard, column), flat_device(dp, (shard + step(dp)) % count, column))
        for dp in range(2)
        for shard in range(count)
        for column in range(x_size * yl_size)
    ]


def ring_pairs(step):
    return shift_pairs(lambda dp: step(dp) * yh_size)


def swap_cores(value):
    return lax.ppermute(value, "dp", [(0, 1), (1, 0)])


def spread(value, axis, count):
    copies = jnp.broadcast_to(value[None], (count,) + value.shape)
    parts = lax.all_to_all(copies, axis, 0, 0)
    return parts.reshape(count * value.shape[0], value.shape[1])


def rotated(values, cosine, sine):
    return values * cosine + pltpu.roll(values, values.shape[-1] // 2, 1) * sine


def part_kernel(order, *refs, alone, both, carried):
    refs = list(refs)
    take = lambda count: [refs.pop(0) for _ in range(count)]
    mine, other = take(alone + both), take(both)
    weights = take(alone + both)
    totals = take(2) if carried else None
    out_mine, out_other = refs
    sums = [totals[0][...], totals[1][...]] if carried else [0.0, 0.0]
    for i, weight in enumerate(weights):
        sums[0] = sums[0] + jnp.dot(
            mine[i][...], weight[...], preferred_element_type=jnp.float32
        )
        if i >= alone:
            sums[1] = sums[1] + jnp.dot(
                other[i - alone][...], weight[...], preferred_element_type=jnp.float32
            )
    out_mine[...] = sums[0]
    out_other[...] = sums[1]


def project_part(order, mine, other, alone, both, totals, name):
    rows = mine.shape[0]
    steps = 2
    part = rows // steps
    weights = alone + both
    depth, columns = weights[0].shape
    tokens = lambda place: pl.BlockSpec((part, depth), lambda i, order: (i, order[place]))
    out = pl.BlockSpec((part, columns), lambda i, order: (i, 0))
    places = list(range(len(weights)))
    work = 2 * rows * depth * columns * (len(alone) + 2 * len(both))
    return pl.pallas_call(
        functools.partial(
            part_kernel, alone=len(alone), both=len(both), carried=bool(totals)
        ),
        grid_spec=pltpu.PrefetchScalarGridSpec(
            num_scalar_prefetch=1,
            grid=(steps,),
            in_specs=[tokens(place) for place in places + places[len(alone) :]]
            + [pl.BlockSpec((depth, columns), lambda i, order: (0, 0))] * len(weights)
            + [out] * len(totals),
            out_specs=[out, out],
        ),
        out_shape=[jax.ShapeDtypeStruct((rows, columns), jnp.float32)] * 2,
        compiler_params=pltpu.CompilerParams(vmem_limit_bytes=vmem_bytes),
        cost_estimate=pl.CostEstimate(
            flops=work, bytes_accessed=work // 256, transcendentals=0
        ),
        name=name,
    )(order, *[mine] * len(weights), *[other] * len(both), *weights, *totals)


def finish_kernel(
    scalars, mine, other, weight, total_mine, total_other, cosine, sine, out_mine, out_other, *, part
):
    head_dim = cosine.shape[1]
    for source, total, out in ((mine, total_mine, out_mine), (other, total_other, out_other)):
        value = total[...] + jnp.dot(
            source[...], weight[...], preferred_element_type=jnp.float32
        )
        for head in range(out.shape[1] // head_dim):
            columns = slice(head * head_dim, (head + 1) * head_dim)
            turned = rotated(value[:, columns], cosine[...], sine[...])
            if part == "kv":
                turned = jnp.where(scalars[1] == 0, turned, value[:, columns])
            out[:, columns] = turned.astype(out.dtype)


def finish(scalars, mine, other, weight, totals, cosine, sine, columns, place, part):
    rows, depth = mine.shape[0], weight.shape[0]
    head_dim = cosine.shape[1]
    tokens = pl.BlockSpec((rows, depth), lambda i, scalars: (0, scalars[0]))
    total = pl.BlockSpec((rows, columns), lambda i, scalars: (0, place))
    table = pl.BlockSpec((rows, head_dim), lambda i, scalars: (0, 0))
    out = pl.BlockSpec((rows, columns), lambda i, scalars: (0, 0))
    return pl.pallas_call(
        functools.partial(finish_kernel, part=part),
        grid_spec=pltpu.PrefetchScalarGridSpec(
            num_scalar_prefetch=1,
            grid=(1,),
            in_specs=[
                tokens,
                tokens,
                pl.BlockSpec((depth, columns), lambda i, scalars: (0, place)),
                total,
                total,
                table,
                table,
            ],
            out_specs=[out, out],
        ),
        out_shape=[jax.ShapeDtypeStruct((rows, columns), jnp.bfloat16)] * 2,
        compiler_params=pltpu.CompilerParams(vmem_limit_bytes=vmem_bytes),
        cost_estimate=pl.CostEstimate(
            flops=4 * rows * depth * columns,
            bytes_accessed=4 * rows * depth + 8 * rows * columns,
            transcendentals=0,
        ),
        name=part + "_finish",
    )(scalars, mine, other, weight, *totals, cosine, sine)


def score_pieces(queries, start, pieces, first):
    head_dim = queries.shape[1]
    scale = math.log2(math.e) / math.sqrt(head_dim)
    contract = (((1,), (1,)), ((), ()))
    scores = []
    for block, low, high, place in pieces:
        part = lax.dot_general(
            queries, block[low:high, :head_dim], contract, preferred_element_type=jnp.float32
        )
        column = place + low + lax.broadcasted_iota(jnp.int32, part.shape, 1)
        seen = column >= start
        if high <= first + tile and place == 3 * block.shape[0]:
            row = lax.broadcasted_iota(jnp.int32, part.shape, 0) % tile
            seen = seen & (column <= row + (place + first))
        scores.append(jnp.where(seen, part * scale, masked_score))
    return scores


def gather_pieces(scores, pieces, peak):
    total, result = 0.0, 0.0
    for part, (block, low, high, place) in zip(scores, pieces):
        head_dim = block.shape[1] // 2
        weights = jnp.exp2(part - peak)
        total = total + jnp.sum(weights, axis=1, keepdims=True)
        result = result + jnp.dot(
            weights.astype(jnp.bfloat16),
            block[low:high, head_dim:],
            preferred_element_type=jnp.float32,
        )
    return total, result


def tile_inputs(half, q_mine, q_other, starts, first, head_dim):
    here = slice(first, first + tile)
    queries = jnp.where(half == 0, q_mine[here], q_other[here])
    heads = queries.shape[1] // head_dim
    queries = jnp.concatenate(
        [queries[:, h * head_dim : (h + 1) * head_dim] for h in range(heads)], axis=0
    )
    return queries, jnp.concatenate([starts[here]] * heads, axis=0)


def near_kernel(core, q_mine, q_other, one_three, three_one, own, starts, partial, stats, three, one):
    half = pl.program_id(0)

    @pl.when((half == 0) & (core[0] == 0))
    def _():
        one[...] = one_three[...]
        three[...] = three_one[...]

    @pl.when((half == 0) & (core[0] == 1))
    def _():
        three[...] = one_three[...]
        one[...] = three_one[...]

    rows, head_dim = own.shape[0], own.shape[1] // 2
    for first in range(0, rows, tile):
        queries, start = tile_inputs(half, q_mine, q_other, starts, first, head_dim)
        pieces = [
            (three, first, rows, 0),
            (one, 0, rows, 2 * rows),
            (own, 0, first + tile, 3 * rows),
        ]
        scores = score_pieces(queries, start, pieces, first)
        peak = functools.reduce(
            jnp.maximum, [jnp.max(part, axis=1, keepdims=True) for part in scores]
        )
        total, result = gather_pieces(scores, pieces, peak)
        height = queries.shape[0]
        place = slice(first // tile * height, (first // tile + 1) * height)
        partial[place] = result
        lane = lax.broadcasted_iota(jnp.int32, (height, head_dim), 1)
        stats[place] = jnp.where(lane < head_dim // 2, peak, total)


def last_kernel(core, q_mine, q_other, two, starts, partial, stats, out):
    half = pl.program_id(0)
    rows, head_dim = two.shape[0], two.shape[1] // 2
    for first in range(0, rows, tile):
        queries, start = tile_inputs(half, q_mine, q_other, starts, first, head_dim)
        height = queries.shape[0]
        pieces = [(two, 0, rows, rows)]
        scores = score_pieces(queries, start, pieces, first)
        place = slice(first // tile * height, (first // tile + 1) * height)
        peak = stats[place, 0:1]
        total = stats[place, head_dim // 2 : head_dim // 2 + 1]
        top = jnp.maximum(peak, jnp.max(scores[0], axis=1, keepdims=True))
        more, result = gather_pieces(scores, pieces, top)
        keep = jnp.exp2(peak - top)
        result = ((partial[place] * keep + result) / (total * keep + more)).astype(out.dtype)
        for h in range(height // tile):
            out[first : first + tile, h * head_dim : (h + 1) * head_dim] = result[
                h * tile : (h + 1) * tile
            ]


def attend(core, q_mine, q_other, one_three, three_one, two, own, starts):
    rows, columns = q_mine.shape
    head_dim = own.shape[1] // 2
    height = rows * columns // head_dim
    whole = lambda array: pl.BlockSpec(array.shape, lambda i, core: (0, 0))
    args = (q_mine, q_other, one_three, three_one, own, starts)
    kept = pl.BlockSpec((height, head_dim), lambda i, core: (i, 0))
    partial, stats = pl.pallas_call(
        near_kernel,
        grid_spec=pltpu.PrefetchScalarGridSpec(
            num_scalar_prefetch=1,
            grid=(2,),
            in_specs=[whole(array) for array in args],
            out_specs=[kept, kept],
            scratch_shapes=[pltpu.VMEM(own.shape, own.dtype)] * 2,
        ),
        out_shape=[jax.ShapeDtypeStruct((2 * height, head_dim), jnp.float32)] * 2,
        compiler_params=pltpu.CompilerParams(vmem_limit_bytes=vmem_bytes),
        cost_estimate=pl.CostEstimate(
            flops=8 * rows * 9 * tile * columns,
            bytes_accessed=16 * rows * columns,
            transcendentals=4 * rows * 9 * tile,
        ),
        name="attend_near",
    )(core, *args)
    args = (q_mine, q_other, two, starts)
    return pl.pallas_call(
        last_kernel,
        grid_spec=pltpu.PrefetchScalarGridSpec(
            num_scalar_prefetch=1,
            grid=(2,),
            in_specs=[whole(array) for array in args] + [kept, kept],
            out_specs=pl.BlockSpec((rows, columns), lambda i, core: (0, (i + core[0]) % 2)),
        ),
        out_shape=jax.ShapeDtypeStruct((rows, 2 * columns), jnp.bfloat16),
        compiler_params=pltpu.CompilerParams(vmem_limit_bytes=vmem_bytes),
        cost_estimate=pl.CostEstimate(
            flops=8 * rows * 4 * tile * columns,
            bytes_accessed=16 * rows * columns,
            transcendentals=4 * rows * 4 * tile,
        ),
        name="attend_last",
    )(core, *args, partial, stats)


def per_device(tokens, lengths, q_weight, kv_weight):
    rows, features = tokens.shape
    head_dim = kv_weight.shape[2] // 2
    core = lax.axis_index("dp")
    plane = lax.axis_index("z")
    shard = plane * yh_size + lax.axis_index("yh")

    depth = q_weight.shape[0]
    half_cols = q_weight.shape[2] // 2
    columns = half_cols + head_dim
    q_half = lax.dynamic_slice_in_dim(q_weight[:, 0], core * half_cols, half_cols, 1)
    kv_half = lax.dynamic_slice_in_dim(kv_weight[:, 0], core * head_dim, head_dim, 1)
    mine = jnp.concatenate([q_half, kv_half], axis=1)
    block = spread(mine, "yh", yh_size)

    positions = shard * rows + jnp.arange(rows, dtype=jnp.int32)
    half = head_dim // 2
    freqs = jnp.exp(
        jnp.arange(half, dtype=jnp.float32) * (-2.0 * math.log(500000.0) / head_dim)
    )
    angle = positions.astype(jnp.float32)[:, None] * freqs[None, :]
    cosine = jnp.concatenate([jnp.cos(angle)] * 2, axis=1)
    sine = jnp.sin(angle)
    sine = jnp.concatenate([-sine, sine], axis=1)
    docs = jnp.arange(lengths.shape[0])
    ends = jnp.sum(jnp.where(docs[None, :] <= docs[:, None], lengths[None, :], 0), axis=1)
    starts = jnp.max(jnp.where(ends[None, :] <= positions[:, None], ends[None, :], 0), axis=1)
    starts = (starts - (shard - 3) * rows)[:, None]

    block, cosine, sine, starts, tokens = lax.optimization_barrier(
        (block, cosine, sine, starts, tokens)
    )
    tokens_other = swap_cores(tokens)
    ahead, back = ring_pairs(lambda dp: 1 - 2 * dp), ring_pairs(lambda dp: 2 * dp - 1)
    aheads, backs = [block], [block]
    for _ in range(z_size // 2 - 1):
        aheads.append(lax.ppermute(aheads[-1], axes, ahead))
        backs.append(lax.ppermute(backs[-1], axes, back))
    far = lax.ppermute(aheads[-1], axes, ahead)
    blocks = [block] + [part for pair in zip(aheads[1:], backs[1:]) for part in pair]
    steps = jnp.array([0, -1, 1, -2, 2, -3, 3, 4], jnp.int32)
    order = (plane + steps * (1 - 2 * core)) % z_size
    totals = project_part(order[:5], tokens, tokens_other, [], blocks[:5], [], "near")
    totals = project_part(
        order[5:7], tokens, tokens_other, [], blocks[5:], list(totals), "farther"
    )

    scalars = jnp.stack([order[-1], core])
    last = (scalars, tokens, tokens_other, far, totals, cosine, sine)
    kv_mine, kv_theirs = finish(*last, head_dim, half_cols // head_dim, "kv")
    kv_other = swap_cores(kv_theirs)
    first = core == 0
    own = jnp.concatenate(
        [lax.select(first, kv_mine, kv_other), lax.select(first, kv_other, kv_mine)], axis=1
    )
    one_three = lax.ppermute(own, axes, shift_pairs(lambda dp: 1 + 2 * dp))
    three_one = lax.ppermute(own, axes, shift_pairs(lambda dp: 3 - 2 * dp))
    two = lax.ppermute(one_three, axes, shift_pairs(lambda dp: 1 - 2 * dp))
    core_index = core.reshape(1).astype(jnp.int32)
    q_mine, q_theirs = finish(*last, half_cols, 0, "q")
    q_other = swap_cores(q_theirs)
    out = attend(core_index, q_mine, q_other, one_three, three_one, two, own, starts)
    return out[:, None]


def solution(mesh):
    split = Mesh(mesh.devices.reshape(2, z_size, yh_size, x_size, yl_size), axes)
    column = P(("z", "yh"), ("x", "yl"), None)
    return jax.shard_map(
        per_device,
        mesh=split,
        in_specs=(P(("dp", "z", "yh"), None), P("dp"), column, column),
        out_specs=P(("dp", "z", "yh"), ("x", "yl"), None),
        check_vma=False,
    )
```

```python
import functools
import math

import jax
import jax.numpy as jnp
from jax import lax
from jax.experimental import pallas as pl
from jax.experimental.pallas import tpu as pltpu
from jax.sharding import Mesh
from jax.sharding import PartitionSpec as P

masked_score = -1e30
axes = ("dp", "z", "yh", "x", "yl")
z_size, yh_size, x_size, yl_size = (8, 4, 4, 2)
vmem_bytes = 48 * 1024 * 1024
tile = 128


def flat_device(dp, shard, column):
    return (dp * z_size * yh_size + shard) * (x_size * yl_size) + column


def shift_pairs(step):
    count = z_size * yh_size
    return [
        (flat_device(dp, shard, column), flat_device(dp, (shard + step(dp)) % count, column))
        for dp in range(2)
        for shard in range(count)
        for column in range(x_size * yl_size)
    ]


def ring_pairs(step):
    return shift_pairs(lambda dp: step(dp) * yh_size)


def swap_cores(value):
    return lax.ppermute(value, "dp", [(0, 1), (1, 0)])


def spread(value, axis, count):
    copies = jnp.broadcast_to(value[None], (count,) + value.shape)
    parts = lax.all_to_all(copies, axis, 0, 0)
    return parts.reshape(count * value.shape[0], value.shape[1])


def rotated(values, cosine, sine):
    return values * cosine + pltpu.roll(values, values.shape[-1] // 2, 1) * sine


def part_kernel(order, *refs, plan):
    refs = list(refs)
    take = lambda count: [refs.pop(0) for _ in range(count)]
    weights = take(1 + max(max(use) for use, _ in plan))
    inputs = [(take(len(use)), use, take(int(carried))) for use, carried in plan]
    for (tokens, use, carried), out in zip(inputs, refs):
        total = carried[0][...] if carried else 0.0
        for part, i in zip(tokens, use):
            total = total + jnp.dot(part[...], weights[i][...], preferred_element_type=jnp.float32)
        out[...] = total


def project_part(order, blocks, results, name):
    rows = results[0][0].shape[0]
    steps = 2
    part = rows // steps
    depth, columns = blocks[0].shape
    tokens = lambda place: pl.BlockSpec((part, depth), lambda i, order: (i, order[place]))
    out = pl.BlockSpec((part, columns), lambda i, order: (i, 0))
    specs = [pl.BlockSpec((depth, columns), lambda i, order: (0, 0))] * len(blocks)
    args = list(blocks)
    for source, use, carried in results:
        specs += [tokens(place) for place in use] + [out] * (carried is not None)
        args += [source] * len(use) + [carried] * (carried is not None)
    work = 2 * rows * depth * columns * sum(len(use) for _, use, _ in results)
    return pl.pallas_call(
        functools.partial(
            part_kernel, plan=[(use, carried is not None) for _, use, carried in results]
        ),
        grid_spec=pltpu.PrefetchScalarGridSpec(
            num_scalar_prefetch=1,
            grid=(steps,),
            in_specs=specs,
            out_specs=[out] * len(results),
        ),
        out_shape=[jax.ShapeDtypeStruct((rows, columns), jnp.float32)] * len(results),
        compiler_params=pltpu.CompilerParams(vmem_limit_bytes=vmem_bytes),
        cost_estimate=pl.CostEstimate(
            flops=work, bytes_accessed=work // 256, transcendentals=0
        ),
        name=name,
    )(order, *args)


def finish_kernel(
    scalars, mine, other, weight, total_mine, total_other, cosine, sine, out_mine, out_other
):
    head_dim = cosine.shape[1]
    heads = weight.shape[1] // head_dim
    for source, total, out in ((mine, total_mine, out_mine), (other, total_other, out_other)):
        value = total[...] + jnp.dot(
            source[...], weight[...], preferred_element_type=jnp.float32
        )
        for head in range(heads):
            columns = slice(head * head_dim, (head + 1) * head_dim)
            turned = rotated(value[:, columns], cosine[...], sine[...])
            if head == heads - 1:
                turned = jnp.where(scalars[1] == 0, turned, value[:, columns])
            out[:, columns] = turned.astype(out.dtype)


def finish(scalars, mine, other, weight, totals, cosine, sine):
    rows, (depth, columns) = mine.shape[0], weight.shape
    steps = 2
    part = rows // steps
    head_dim = cosine.shape[1]
    tokens = pl.BlockSpec((part, depth), lambda i, scalars: (i, scalars[0]))
    table = pl.BlockSpec((part, head_dim), lambda i, scalars: (i, 0))
    out = pl.BlockSpec((part, columns), lambda i, scalars: (i, 0))
    return pl.pallas_call(
        finish_kernel,
        grid_spec=pltpu.PrefetchScalarGridSpec(
            num_scalar_prefetch=1,
            grid=(steps,),
            in_specs=[
                tokens,
                tokens,
                pl.BlockSpec((depth, columns), lambda i, scalars: (0, 0)),
                out,
                out,
                table,
                table,
            ],
            out_specs=[out, out],
        ),
        out_shape=[jax.ShapeDtypeStruct((rows, columns), jnp.bfloat16)] * 2,
        compiler_params=pltpu.CompilerParams(vmem_limit_bytes=vmem_bytes),
        cost_estimate=pl.CostEstimate(
            flops=4 * rows * depth * columns,
            bytes_accessed=4 * rows * depth + 8 * rows * columns,
            transcendentals=0,
        ),
        name="finish",
    )(scalars, mine, other, weight, *totals, cosine, sine)


def score_pieces(queries, start, pieces, first):
    head_dim = queries.shape[1]
    scale = math.log2(math.e) / math.sqrt(head_dim)
    contract = (((1,), (1,)), ((), ()))
    scores = []
    for block, low, high, place in pieces:
        part = lax.dot_general(
            queries, block[low:high, :head_dim], contract, preferred_element_type=jnp.float32
        )
        column = place + low + lax.broadcasted_iota(jnp.int32, part.shape, 1)
        seen = column >= start
        if high <= first + tile and place == 3 * block.shape[0]:
            row = lax.broadcasted_iota(jnp.int32, part.shape, 0) % tile
            seen = seen & (column <= row + (place + first))
        scores.append(jnp.where(seen, part * scale, masked_score))
    return scores


def gather_pieces(scores, pieces, peak):
    total, result = 0.0, 0.0
    for part, (block, low, high, place) in zip(scores, pieces):
        head_dim = block.shape[1] // 2
        weights = jnp.exp2(part - peak)
        total = total + jnp.sum(weights, axis=1, keepdims=True)
        result = result + jnp.dot(
            weights.astype(jnp.bfloat16),
            block[low:high, head_dim:],
            preferred_element_type=jnp.float32,
        )
    return total, result


def tile_inputs(half, q_mine, q_other, starts, first, head_dim):
    here = slice(first, first + tile)
    queries = jnp.where(half == 0, q_mine[here], q_other[here])
    heads = queries.shape[1] // head_dim
    queries = jnp.concatenate(
        [queries[:, h * head_dim : (h + 1) * head_dim] for h in range(heads)], axis=0
    )
    return queries, jnp.concatenate([starts[here]] * heads, axis=0)


def near_kernel(core, q_mine, q_other, one_three, three_one, own, starts, partial, stats, three, one):
    half = pl.program_id(0)

    @pl.when((half == 0) & (core[0] == 0))
    def _():
        one[...] = one_three[...]
        three[...] = three_one[...]

    @pl.when((half == 0) & (core[0] == 1))
    def _():
        three[...] = one_three[...]
        one[...] = three_one[...]

    rows, head_dim = own.shape[0], own.shape[1] // 2
    for first in range(0, rows, tile):
        queries, start = tile_inputs(half, q_mine, q_other, starts, first, head_dim)
        pieces = [
            (three, first, rows, 0),
            (one, 0, rows, 2 * rows),
            (own, 0, first + tile, 3 * rows),
        ]
        scores = score_pieces(queries, start, pieces, first)
        peak = functools.reduce(
            jnp.maximum, [jnp.max(part, axis=1, keepdims=True) for part in scores]
        )
        total, result = gather_pieces(scores, pieces, peak)
        height = queries.shape[0]
        place = slice(first // tile * height, (first // tile + 1) * height)
        partial[place] = result
        lane = lax.broadcasted_iota(jnp.int32, (height, head_dim), 1)
        stats[place] = jnp.where(lane < head_dim // 2, peak, total)


def last_kernel(core, q_mine, q_other, two, starts, partial, stats, out):
    half = pl.program_id(0)
    rows, head_dim = two.shape[0], two.shape[1] // 2
    for first in range(0, rows, tile):
        queries, start = tile_inputs(half, q_mine, q_other, starts, first, head_dim)
        height = queries.shape[0]
        pieces = [(two, 0, rows, rows)]
        scores = score_pieces(queries, start, pieces, first)
        place = slice(first // tile * height, (first // tile + 1) * height)
        peak = stats[place, 0:1]
        total = stats[place, head_dim // 2 : head_dim // 2 + 1]
        top = jnp.maximum(peak, jnp.max(scores[0], axis=1, keepdims=True))
        more, result = gather_pieces(scores, pieces, top)
        keep = jnp.exp2(peak - top)
        result = ((partial[place] * keep + result) / (total * keep + more)).astype(out.dtype)
        for h in range(height // tile):
            out[first : first + tile, h * head_dim : (h + 1) * head_dim] = result[
                h * tile : (h + 1) * tile
            ]


def attend(core, q_mine, q_other, columns, one_three, three_one, two, own, starts):
    rows = own.shape[0]
    head_dim = own.shape[1] // 2
    height = rows * columns // head_dim
    whole = lambda array: pl.BlockSpec(array.shape, lambda i, core: (0, 0))
    half = pl.BlockSpec((rows, columns), lambda i, core: (0, 0))
    args = (q_mine, q_other, one_three, three_one, own, starts)
    kept = pl.BlockSpec((height, head_dim), lambda i, core: (i, 0))
    partial, stats = pl.pallas_call(
        near_kernel,
        grid_spec=pltpu.PrefetchScalarGridSpec(
            num_scalar_prefetch=1,
            grid=(2,),
            in_specs=[half, half] + [whole(array) for array in args[2:]],
            out_specs=[kept, kept],
            scratch_shapes=[pltpu.VMEM(own.shape, own.dtype)] * 2,
        ),
        out_shape=[jax.ShapeDtypeStruct((2 * height, head_dim), jnp.float32)] * 2,
        compiler_params=pltpu.CompilerParams(vmem_limit_bytes=vmem_bytes),
        cost_estimate=pl.CostEstimate(
            flops=8 * rows * 9 * tile * columns,
            bytes_accessed=16 * rows * columns,
            transcendentals=4 * rows * 9 * tile,
        ),
        name="attend_near",
    )(core, *args)
    args = (q_mine, q_other, two, starts)
    return pl.pallas_call(
        last_kernel,
        grid_spec=pltpu.PrefetchScalarGridSpec(
            num_scalar_prefetch=1,
            grid=(2,),
            in_specs=[half, half] + [whole(array) for array in args[2:]] + [kept, kept],
            out_specs=pl.BlockSpec((rows, columns), lambda i, core: (0, (i + core[0]) % 2)),
        ),
        out_shape=jax.ShapeDtypeStruct((rows, 2 * columns), jnp.bfloat16),
        compiler_params=pltpu.CompilerParams(vmem_limit_bytes=vmem_bytes),
        cost_estimate=pl.CostEstimate(
            flops=8 * rows * 4 * tile * columns,
            bytes_accessed=16 * rows * columns,
            transcendentals=4 * rows * 4 * tile,
        ),
        name="attend_last",
    )(core, *args, partial, stats)


def per_device(tokens, lengths, q_weight, kv_weight):
    rows, features = tokens.shape
    head_dim = kv_weight.shape[2] // 2
    core = lax.axis_index("dp")
    plane = lax.axis_index("z")
    shard = plane * yh_size + lax.axis_index("yh")

    depth = q_weight.shape[0]
    half_cols = q_weight.shape[2] // 2
    columns = half_cols + head_dim
    q_half = lax.dynamic_slice_in_dim(q_weight[:, 0], core * half_cols, half_cols, 1)
    kv_half = lax.dynamic_slice_in_dim(kv_weight[:, 0], core * head_dim, head_dim, 1)
    mine = jnp.concatenate([q_half, kv_half], axis=1)
    block = spread(mine, "yh", yh_size)

    positions = shard * rows + jnp.arange(rows, dtype=jnp.int32)
    half = head_dim // 2
    freqs = jnp.exp(
        jnp.arange(half, dtype=jnp.float32) * (-2.0 * math.log(500000.0) / head_dim)
    )
    angle = positions.astype(jnp.float32)[:, None] * freqs[None, :]
    cosine = jnp.concatenate([jnp.cos(angle)] * 2, axis=1)
    sine = jnp.sin(angle)
    sine = jnp.concatenate([-sine, sine], axis=1)
    docs = jnp.arange(lengths.shape[0])
    ends = jnp.sum(jnp.where(docs[None, :] <= docs[:, None], lengths[None, :], 0), axis=1)
    starts = jnp.max(jnp.where(ends[None, :] <= positions[:, None], ends[None, :], 0), axis=1)
    starts = (starts - (shard - 3) * rows)[:, None]

    block, cosine, sine, starts, tokens = lax.optimization_barrier(
        (block, cosine, sine, starts, tokens)
    )
    tokens_other = swap_cores(tokens)
    ahead, back = ring_pairs(lambda dp: 1 - 2 * dp), ring_pairs(lambda dp: 2 * dp - 1)
    send_ahead = lambda value: lax.ppermute(value, axes, ahead)
    send_back = lambda value: lax.ppermute(value, axes, back)
    steps = jnp.array([0, -1, 1, -2, 2, -3, 3, 4], jnp.int32)
    order = (plane + steps * (1 - 2 * core)) % z_size
    ahead1, back1 = send_ahead(block), send_back(block)
    ahead2, back2 = send_ahead(ahead1), send_back(back1)
    blocks = [block, ahead1, back1]
    (total,) = project_part(order, blocks, [(tokens, [0, 1, 2], None)], "first")
    ahead2, total = lax.optimization_barrier((ahead2, total))
    ahead3, back3 = send_ahead(ahead2), send_back(back2)
    blocks += [ahead2, back2]
    totals = project_part(
        order, blocks, [(tokens, [3, 4], total), (tokens_other, [0, 1, 2, 3, 4], None)], "second"
    )
    ahead3, *totals = lax.optimization_barrier((ahead3, *totals))
    far = send_ahead(ahead3)
    totals = project_part(
        order[5:7],
        [ahead3, back3],
        [(tokens, [0, 1], totals[0]), (tokens_other, [0, 1], totals[1])],
        "third",
    )
    scalars = jnp.stack([order[7], core])
    mine, theirs = finish(scalars, tokens, tokens_other, far, totals, cosine, sine)
    other = swap_cores(theirs)
    first = core == 0
    kv_mine, kv_other = mine[:, half_cols:], other[:, half_cols:]
    own = jnp.concatenate(
        [lax.select(first, kv_mine, kv_other), lax.select(first, kv_other, kv_mine)], axis=1
    )
    one_three = lax.ppermute(own, axes, shift_pairs(lambda dp: 1 + 2 * dp))
    three_one = lax.ppermute(own, axes, shift_pairs(lambda dp: 3 - 2 * dp))
    two = lax.ppermute(one_three, axes, shift_pairs(lambda dp: 1 - 2 * dp))
    core_index = core.reshape(1).astype(jnp.int32)
    out = attend(core_index, mine, other, half_cols, one_three, three_one, two, own, starts)
    return out[:, None]


def solution(mesh):
    split = Mesh(mesh.devices.reshape(2, z_size, yh_size, x_size, yl_size), axes)
    column = P(("z", "yh"), ("x", "yl"), None)
    return jax.shard_map(
        per_device,
        mesh=split,
        in_specs=(P(("dp", "z", "yh"), None), P("dp"), column, column),
        out_specs=P(("dp", "z", "yh"), ("x", "yl"), None),
        check_vma=False,
    )
```

```python
import functools
import math

import jax
import jax.numpy as jnp
from jax import lax
from jax.experimental import pallas as pl
from jax.experimental.pallas import tpu as pltpu
from jax.sharding import Mesh
from jax.sharding import PartitionSpec as P

masked_score = -1e30
axes = ("dp", "z", "yh", "x", "yl")
z_size, yh_size, x_size, yl_size = (8, 4, 4, 2)
vmem_bytes = 48 * 1024 * 1024
tile = 128


def flat_device(dp, shard, column):
    return (dp * z_size * yh_size + shard) * (x_size * yl_size) + column


def shift_pairs(step):
    count = z_size * yh_size
    return [
        (flat_device(dp, shard, column), flat_device(dp, (shard + step(dp)) % count, column))
        for dp in range(2)
        for shard in range(count)
        for column in range(x_size * yl_size)
    ]


def ring_pairs(step):
    return shift_pairs(lambda dp: step(dp) * yh_size)


def swap_cores(value):
    return lax.ppermute(value, "dp", [(0, 1), (1, 0)])


def spread(value, axis, count):
    copies = jnp.broadcast_to(value[None], (count,) + value.shape)
    parts = lax.all_to_all(copies, axis, 0, 0)
    return parts.reshape(count * value.shape[0], value.shape[1])


def rotated(values, cosine, sine):
    return values * cosine + pltpu.roll(values, values.shape[-1] // 2, 1) * sine


def part_kernel(order, *refs, plan):
    refs = list(refs)
    take = lambda count: [refs.pop(0) for _ in range(count)]
    weights = take(1 + max(max(use) for use, _ in plan))
    inputs = [(take(len(use)), use, take(int(carried))) for use, carried in plan]
    for (tokens, use, carried), out in zip(inputs, refs):
        total = carried[0][...] if carried else 0.0
        for part, i in zip(tokens, use):
            total = total + jnp.dot(part[...], weights[i][...], preferred_element_type=jnp.float32)
        out[...] = total


def project_part(order, blocks, results, name):
    rows = results[0][0].shape[0]
    steps = 2
    part = rows // steps
    depth, columns = blocks[0].shape
    tokens = lambda place: pl.BlockSpec((part, depth), lambda i, order: (i, order[place]))
    out = pl.BlockSpec((part, columns), lambda i, order: (i, 0))
    specs = [pl.BlockSpec((depth, columns), lambda i, order: (0, 0))] * len(blocks)
    args = list(blocks)
    for source, use, carried in results:
        specs += [tokens(place) for place in use] + [out] * (carried is not None)
        args += [source] * len(use) + [carried] * (carried is not None)
    work = 2 * rows * depth * columns * sum(len(use) for _, use, _ in results)
    return pl.pallas_call(
        functools.partial(
            part_kernel, plan=[(use, carried is not None) for _, use, carried in results]
        ),
        grid_spec=pltpu.PrefetchScalarGridSpec(
            num_scalar_prefetch=1,
            grid=(steps,),
            in_specs=specs,
            out_specs=[out] * len(results),
        ),
        out_shape=[jax.ShapeDtypeStruct((rows, columns), jnp.float32)] * len(results),
        compiler_params=pltpu.CompilerParams(vmem_limit_bytes=vmem_bytes),
        cost_estimate=pl.CostEstimate(
            flops=work, bytes_accessed=work // 256, transcendentals=0
        ),
        name=name,
    )(order, *args)


def finish_kernel(
    scalars, mine, other, weight, total_mine, total_other, cosine, sine, out_mine, out_other
):
    head_dim = cosine.shape[1]
    heads = weight.shape[1] // head_dim
    for source, total, out in ((mine, total_mine, out_mine), (other, total_other, out_other)):
        value = total[...] + jnp.dot(
            source[...], weight[...], preferred_element_type=jnp.float32
        )
        for head in range(heads):
            columns = slice(head * head_dim, (head + 1) * head_dim)
            turned = rotated(value[:, columns], cosine[...], sine[...])
            if head == heads - 1:
                turned = jnp.where(scalars[1] == 0, turned, value[:, columns])
            out[:, columns] = turned.astype(out.dtype)


def finish(scalars, mine, other, weight, totals, cosine, sine):
    rows, (depth, columns) = mine.shape[0], weight.shape
    steps = 2
    part = rows // steps
    head_dim = cosine.shape[1]
    tokens = pl.BlockSpec((part, depth), lambda i, scalars: (i, scalars[0]))
    table = pl.BlockSpec((part, head_dim), lambda i, scalars: (i, 0))
    out = pl.BlockSpec((part, columns), lambda i, scalars: (i, 0))
    return pl.pallas_call(
        finish_kernel,
        grid_spec=pltpu.PrefetchScalarGridSpec(
            num_scalar_prefetch=1,
            grid=(steps,),
            in_specs=[
                tokens,
                tokens,
                pl.BlockSpec((depth, columns), lambda i, scalars: (0, 0)),
                out,
                out,
                table,
                table,
            ],
            out_specs=[out, out],
        ),
        out_shape=[jax.ShapeDtypeStruct((rows, columns), jnp.bfloat16)] * 2,
        compiler_params=pltpu.CompilerParams(vmem_limit_bytes=vmem_bytes),
        cost_estimate=pl.CostEstimate(
            flops=4 * rows * depth * columns,
            bytes_accessed=4 * rows * depth + 8 * rows * columns,
            transcendentals=0,
        ),
        name="finish",
    )(scalars, mine, other, weight, *totals, cosine, sine)


def score_pieces(queries, start, pieces, first):
    head_dim = queries.shape[1]
    scale = math.log2(math.e) / math.sqrt(head_dim)
    contract = (((1,), (1,)), ((), ()))
    scores = []
    for block, low, high, place in pieces:
        part = lax.dot_general(
            queries, block[low:high, :head_dim], contract, preferred_element_type=jnp.float32
        )
        column = place + low + lax.broadcasted_iota(jnp.int32, part.shape, 1)
        seen = column >= start
        if high <= first + tile and place == 3 * block.shape[0]:
            row = lax.broadcasted_iota(jnp.int32, part.shape, 0) % tile
            seen = seen & (column <= row + (place + first))
        scores.append(jnp.where(seen, part * scale, masked_score))
    return scores


def gather_pieces(scores, pieces, peak):
    total, result = 0.0, 0.0
    for part, (block, low, high, place) in zip(scores, pieces):
        head_dim = block.shape[1] // 2
        weights = jnp.exp2(part - peak)
        total = total + jnp.sum(weights, axis=1, keepdims=True)
        result = result + jnp.dot(
            weights.astype(jnp.bfloat16),
            block[low:high, head_dim:],
            preferred_element_type=jnp.float32,
        )
    return total, result


def tile_inputs(half, q_mine, q_other, starts, first, head_dim):
    here = slice(first, first + tile)
    queries = jnp.where(half == 0, q_mine[here], q_other[here])
    heads = queries.shape[1] // head_dim
    queries = jnp.concatenate(
        [queries[:, h * head_dim : (h + 1) * head_dim] for h in range(heads)], axis=0
    )
    return queries, jnp.concatenate([starts[here]] * heads, axis=0)


def near_kernel(core, q_mine, q_other, one_three, three_one, own, starts, partial, stats, three, one):
    half = pl.program_id(0)

    @pl.when((half == 0) & (core[0] == 0))
    def _():
        one[...] = one_three[...]
        three[...] = three_one[...]

    @pl.when((half == 0) & (core[0] == 1))
    def _():
        three[...] = one_three[...]
        one[...] = three_one[...]

    rows, head_dim = own.shape[0], own.shape[1] // 2
    for first in range(0, rows, tile):
        queries, start = tile_inputs(half, q_mine, q_other, starts, first, head_dim)
        pieces = [
            (three, first, rows, 0),
            (one, 0, rows, 2 * rows),
            (own, 0, first + tile, 3 * rows),
        ]
        scores = score_pieces(queries, start, pieces, first)
        peak = functools.reduce(
            jnp.maximum, [jnp.max(part, axis=1, keepdims=True) for part in scores]
        )
        total, result = gather_pieces(scores, pieces, peak)
        height = queries.shape[0]
        place = slice(first // tile * height, (first // tile + 1) * height)
        partial[place] = result
        lane = lax.broadcasted_iota(jnp.int32, (height, head_dim), 1)
        stats[place] = jnp.where(lane < head_dim // 2, peak, total)


def last_kernel(core, q_mine, q_other, two, starts, partial, stats, out):
    half = pl.program_id(0)
    rows, head_dim = two.shape[0], two.shape[1] // 2
    for first in range(0, rows, tile):
        queries, start = tile_inputs(half, q_mine, q_other, starts, first, head_dim)
        height = queries.shape[0]
        pieces = [(two, 0, rows, rows)]
        scores = score_pieces(queries, start, pieces, first)
        place = slice(first // tile * height, (first // tile + 1) * height)
        peak = stats[place, 0:1]
        total = stats[place, head_dim // 2 : head_dim // 2 + 1]
        top = jnp.maximum(peak, jnp.max(scores[0], axis=1, keepdims=True))
        more, result = gather_pieces(scores, pieces, top)
        keep = jnp.exp2(peak - top)
        result = ((partial[place] * keep + result) / (total * keep + more)).astype(out.dtype)
        for h in range(height // tile):
            out[first : first + tile, h * head_dim : (h + 1) * head_dim] = result[
                h * tile : (h + 1) * tile
            ]


def attend(core, q_mine, q_other, columns, one_three, three_one, two, own, starts):
    rows = own.shape[0]
    head_dim = own.shape[1] // 2
    height = rows * columns // head_dim
    whole = lambda array: pl.BlockSpec(array.shape, lambda i, core: (0, 0))
    half = pl.BlockSpec((rows, columns), lambda i, core: (0, 0))
    args = (q_mine, q_other, one_three, three_one, own, starts)
    kept = pl.BlockSpec((height, head_dim), lambda i, core: (i, 0))
    partial, stats = pl.pallas_call(
        near_kernel,
        grid_spec=pltpu.PrefetchScalarGridSpec(
            num_scalar_prefetch=1,
            grid=(2,),
            in_specs=[half, half] + [whole(array) for array in args[2:]],
            out_specs=[kept, kept],
            scratch_shapes=[pltpu.VMEM(own.shape, own.dtype)] * 2,
        ),
        out_shape=[jax.ShapeDtypeStruct((2 * height, head_dim), jnp.float32)] * 2,
        compiler_params=pltpu.CompilerParams(vmem_limit_bytes=vmem_bytes),
        cost_estimate=pl.CostEstimate(
            flops=8 * rows * 9 * tile * columns,
            bytes_accessed=16 * rows * columns,
            transcendentals=4 * rows * 9 * tile,
        ),
        name="attend_near",
    )(core, *args)
    args = (q_mine, q_other, two, starts)
    return pl.pallas_call(
        last_kernel,
        grid_spec=pltpu.PrefetchScalarGridSpec(
            num_scalar_prefetch=1,
            grid=(2,),
            in_specs=[half, half] + [whole(array) for array in args[2:]] + [kept, kept],
            out_specs=pl.BlockSpec((rows, columns), lambda i, core: (0, (i + core[0]) % 2)),
        ),
        out_shape=jax.ShapeDtypeStruct((rows, 2 * columns), jnp.bfloat16),
        compiler_params=pltpu.CompilerParams(vmem_limit_bytes=vmem_bytes),
        cost_estimate=pl.CostEstimate(
            flops=8 * rows * 4 * tile * columns,
            bytes_accessed=16 * rows * columns,
            transcendentals=4 * rows * 4 * tile,
        ),
        name="attend_last",
    )(core, *args, partial, stats)


def per_device(tokens, lengths, q_weight, kv_weight):
    rows, features = tokens.shape
    head_dim = kv_weight.shape[2] // 2
    core = lax.axis_index("dp")
    plane = lax.axis_index("z")
    shard = plane * yh_size + lax.axis_index("yh")

    depth = q_weight.shape[0]
    half_cols = q_weight.shape[2] // 2
    columns = half_cols + head_dim
    q_half = lax.dynamic_slice_in_dim(q_weight[:, 0], core * half_cols, half_cols, 1)
    kv_half = lax.dynamic_slice_in_dim(kv_weight[:, 0], core * head_dim, head_dim, 1)
    mine = jnp.concatenate([q_half, kv_half], axis=1)
    block = spread(mine, "yh", yh_size)

    positions = shard * rows + jnp.arange(rows, dtype=jnp.int32)
    half = head_dim // 2
    freqs = jnp.exp(
        jnp.arange(half, dtype=jnp.float32) * (-2.0 * math.log(500000.0) / head_dim)
    )
    angle = positions.astype(jnp.float32)[:, None] * freqs[None, :]
    cosine = jnp.concatenate([jnp.cos(angle)] * 2, axis=1)
    sine = jnp.sin(angle)
    sine = jnp.concatenate([-sine, sine], axis=1)
    docs = jnp.arange(lengths.shape[0])
    ends = jnp.sum(jnp.where(docs[None, :] <= docs[:, None], lengths[None, :], 0), axis=1)
    starts = jnp.max(jnp.where(ends[None, :] <= positions[:, None], ends[None, :], 0), axis=1)
    starts = (starts - (shard - 3) * rows)[:, None]

    block, cosine, sine, starts, tokens = lax.optimization_barrier(
        (block, cosine, sine, starts, tokens)
    )
    tokens_other = swap_cores(tokens)
    ahead, back = ring_pairs(lambda dp: 1 - 2 * dp), ring_pairs(lambda dp: 2 * dp - 1)
    send_ahead = lambda value: lax.ppermute(value, axes, ahead)
    send_back = lambda value: lax.ppermute(value, axes, back)
    steps = jnp.array([0, -1, 1, -2, 2, -3, 3, 4], jnp.int32)
    order = (plane + steps * (1 - 2 * core)) % z_size
    ahead1, back1 = send_ahead(block), send_back(block)
    ahead2, back2 = send_ahead(ahead1), send_back(back1)
    blocks = [block, ahead1, back1]
    (total,) = project_part(order, blocks, [(tokens, [0, 1, 2], None)], "first")
    ahead2, total = lax.optimization_barrier((ahead2, total))
    ahead3, back3 = send_ahead(ahead2), send_back(back2)
    far = lax.ppermute(ahead2, axes, ring_pairs(lambda dp: 2 - 4 * dp))
    blocks += [ahead2, back2]
    totals = project_part(
        order, blocks, [(tokens, [3, 4], total), (tokens_other, [0, 1, 2, 3, 4], None)], "second"
    )
    totals = project_part(
        order[5:7],
        [ahead3, back3],
        [(tokens, [0, 1], totals[0]), (tokens_other, [0, 1], totals[1])],
        "third",
    )
    scalars = jnp.stack([order[7], core])
    mine, theirs = finish(scalars, tokens, tokens_other, far, totals, cosine, sine)
    other = swap_cores(theirs)
    first = core == 0
    kv_mine, kv_other = mine[:, half_cols:], other[:, half_cols:]
    own = jnp.concatenate(
        [lax.select(first, kv_mine, kv_other), lax.select(first, kv_other, kv_mine)], axis=1
    )
    one_three = lax.ppermute(own, axes, shift_pairs(lambda dp: 1 + 2 * dp))
    three_one = lax.ppermute(own, axes, shift_pairs(lambda dp: 3 - 2 * dp))
    two = lax.ppermute(one_three, axes, shift_pairs(lambda dp: 1 - 2 * dp))
    core_index = core.reshape(1).astype(jnp.int32)
    out = attend(core_index, mine, other, half_cols, one_three, three_one, two, own, starts)
    return out[:, None]


def solution(mesh):
    split = Mesh(mesh.devices.reshape(2, z_size, yh_size, x_size, yl_size), axes)
    column = P(("z", "yh"), ("x", "yl"), None)
    return jax.shard_map(
        per_device,
        mesh=split,
        in_specs=(P(("dp", "z", "yh"), None), P("dp"), column, column),
        out_specs=P(("dp", "z", "yh"), ("x", "yl"), None),
        check_vma=False,
    )
```

```python
import functools
import math

import jax
import jax.numpy as jnp
from jax import lax
from jax.experimental import pallas as pl
from jax.experimental.pallas import tpu as pltpu
from jax.sharding import Mesh
from jax.sharding import PartitionSpec as P

masked_score = -1e30
axes = ("dp", "z", "yh", "x", "yl")
z_size, yh_size, x_size, yl_size = (8, 4, 4, 2)
vmem_bytes = 48 * 1024 * 1024
tile = 128


def flat_device(dp, shard, column):
    return (dp * z_size * yh_size + shard) * (x_size * yl_size) + column


def shift_pairs(step):
    count = z_size * yh_size
    return [
        (flat_device(dp, shard, column), flat_device(dp, (shard + step(dp)) % count, column))
        for dp in range(2)
        for shard in range(count)
        for column in range(x_size * yl_size)
    ]


def ring_pairs(step):
    return shift_pairs(lambda dp: step(dp) * yh_size)


def swap_cores(value):
    return lax.ppermute(value, "dp", [(0, 1), (1, 0)])


def spread(value, axis, count):
    copies = jnp.broadcast_to(value[None], (count,) + value.shape)
    parts = lax.all_to_all(copies, axis, 0, 0)
    return parts.reshape(count * value.shape[0], value.shape[1])


def rotated(values, cosine, sine):
    return values * cosine + pltpu.roll(values, values.shape[-1] // 2, 1) * sine


def part_kernel(order, *refs, plan):
    refs = list(refs)
    take = lambda count: [refs.pop(0) for _ in range(count)]
    weights = take(1 + max(max(use) for use, _ in plan))
    inputs = [(take(len(use)), use, take(int(carried))) for use, carried in plan]
    for (tokens, use, carried), out in zip(inputs, refs):
        total = carried[0][...] if carried else 0.0
        for part, i in zip(tokens, use):
            total = total + jnp.dot(part[...], weights[i][...], preferred_element_type=jnp.float32)
        out[...] = total


def project_part(order, blocks, results, name):
    rows = results[0][0].shape[0]
    steps = 2
    part = rows // steps
    depth, columns = blocks[0].shape
    tokens = lambda place: pl.BlockSpec((part, depth), lambda i, order: (i, order[place]))
    out = pl.BlockSpec((part, columns), lambda i, order: (i, 0))
    specs = [pl.BlockSpec((depth, columns), lambda i, order: (0, 0))] * len(blocks)
    args = list(blocks)
    for source, use, carried in results:
        specs += [tokens(place) for place in use] + [out] * (carried is not None)
        args += [source] * len(use) + [carried] * (carried is not None)
    work = 2 * rows * depth * columns * sum(len(use) for _, use, _ in results)
    return pl.pallas_call(
        functools.partial(
            part_kernel, plan=[(use, carried is not None) for _, use, carried in results]
        ),
        grid_spec=pltpu.PrefetchScalarGridSpec(
            num_scalar_prefetch=1,
            grid=(steps,),
            in_specs=specs,
            out_specs=[out] * len(results),
        ),
        out_shape=[jax.ShapeDtypeStruct((rows, columns), jnp.float32)] * len(results),
        compiler_params=pltpu.CompilerParams(vmem_limit_bytes=vmem_bytes),
        cost_estimate=pl.CostEstimate(
            flops=work, bytes_accessed=work // 256, transcendentals=0
        ),
        name=name,
    )(order, *args)


def finish_kernel(
    scalars, mine, other, weight, total_mine, total_other, cosine, sine, out_mine, out_other
):
    head_dim = cosine.shape[1]
    heads = weight.shape[1] // head_dim
    for source, total, out in ((mine, total_mine, out_mine), (other, total_other, out_other)):
        value = total[...] + jnp.dot(
            source[...], weight[...], preferred_element_type=jnp.float32
        )
        for head in range(heads):
            columns = slice(head * head_dim, (head + 1) * head_dim)
            turned = rotated(value[:, columns], cosine[...], sine[...])
            if head == heads - 1:
                turned = jnp.where(scalars[1] == 0, turned, value[:, columns])
            out[:, columns] = turned.astype(out.dtype)


def finish(scalars, mine, other, weight, totals, cosine, sine):
    rows, (depth, columns) = mine.shape[0], weight.shape
    steps = 1
    part = rows // steps
    head_dim = cosine.shape[1]
    tokens = pl.BlockSpec((part, depth), lambda i, scalars: (i, scalars[0]))
    table = pl.BlockSpec((part, head_dim), lambda i, scalars: (i, 0))
    out = pl.BlockSpec((part, columns), lambda i, scalars: (i, 0))
    return pl.pallas_call(
        finish_kernel,
        grid_spec=pltpu.PrefetchScalarGridSpec(
            num_scalar_prefetch=1,
            grid=(steps,),
            in_specs=[
                tokens,
                tokens,
                pl.BlockSpec((depth, columns), lambda i, scalars: (0, 0)),
                out,
                out,
                table,
                table,
            ],
            out_specs=[out, out],
        ),
        out_shape=[jax.ShapeDtypeStruct((rows, columns), jnp.bfloat16)] * 2,
        compiler_params=pltpu.CompilerParams(vmem_limit_bytes=vmem_bytes),
        cost_estimate=pl.CostEstimate(
            flops=4 * rows * depth * columns,
            bytes_accessed=4 * rows * depth + 8 * rows * columns,
            transcendentals=0,
        ),
        name="finish",
    )(scalars, mine, other, weight, *totals, cosine, sine)


def score_pieces(queries, start, pieces, first):
    head_dim = queries.shape[1]
    scale = math.log2(math.e) / math.sqrt(head_dim)
    contract = (((1,), (1,)), ((), ()))
    scores = []
    for block, low, high, place in pieces:
        part = lax.dot_general(
            queries, block[low:high, :head_dim], contract, preferred_element_type=jnp.float32
        )
        column = place + low + lax.broadcasted_iota(jnp.int32, part.shape, 1)
        seen = column >= start
        if high <= first + tile and place == 3 * block.shape[0]:
            row = lax.broadcasted_iota(jnp.int32, part.shape, 0) % tile
            seen = seen & (column <= row + (place + first))
        scores.append(jnp.where(seen, part * scale, masked_score))
    return scores


def gather_pieces(scores, pieces, peak):
    total, result = 0.0, 0.0
    for part, (block, low, high, place) in zip(scores, pieces):
        head_dim = block.shape[1] // 2
        weights = jnp.exp2(part - peak)
        total = total + jnp.sum(weights, axis=1, keepdims=True)
        result = result + jnp.dot(
            weights.astype(jnp.bfloat16),
            block[low:high, head_dim:],
            preferred_element_type=jnp.float32,
        )
    return total, result


def tile_inputs(queries, starts, first, heads, head_dim):
    here = slice(first, first + tile)
    stacked = jnp.concatenate(
        [queries[here, h * head_dim : (h + 1) * head_dim] for h in range(heads)], axis=0
    )
    return stacked, jnp.concatenate([starts[here]] * heads, axis=0)


def near_kernel(
    core, q_mine, q_other, one_three, three_one, own, starts, partial, stats, three, one, *, heads
):
    rows, head_dim = own.shape[0], own.shape[1] // 2

    @pl.when(core[0] == 0)
    def _():
        one[...] = one_three[...]
        three[...] = three_one[...]

    @pl.when(core[0] == 1)
    def _():
        three[...] = one_three[...]
        one[...] = three_one[...]

    height = heads * tile
    for half, q in enumerate((q_mine, q_other)):
        for first in range(0, rows, tile):
            queries, start = tile_inputs(q, starts, first, heads, head_dim)
            pieces = [
                (three, first, rows, 0),
                (one, 0, rows, 2 * rows),
                (own, 0, first + tile, 3 * rows),
            ]
            scores = score_pieces(queries, start, pieces, first)
            peak = functools.reduce(
                jnp.maximum, [jnp.max(part, axis=1, keepdims=True) for part in scores]
            )
            total, result = gather_pieces(scores, pieces, peak)
            base = (half * rows + first) * heads
            place = slice(base, base + height)
            partial[place] = result
            lane = lax.broadcasted_iota(jnp.int32, (height, head_dim), 1)
            stats[place] = jnp.where(lane < head_dim // 2, peak, total)


def last_kernel(core, q_mine, q_other, two, starts, partial, stats, out, *, heads):
    rows, head_dim = two.shape[0], two.shape[1] // 2
    height = heads * tile
    for half, q in enumerate((q_mine, q_other)):
        for first in range(0, rows, tile):
            queries, start = tile_inputs(q, starts, first, heads, head_dim)
            pieces = [(two, 0, rows, rows)]
            scores = score_pieces(queries, start, pieces, first)
            base = (half * rows + first) * heads
            place = slice(base, base + height)
            peak = stats[place, 0:1]
            total = stats[place, head_dim // 2 : head_dim // 2 + 1]
            top = jnp.maximum(peak, jnp.max(scores[0], axis=1, keepdims=True))
            more, result = gather_pieces(scores, pieces, top)
            keep = jnp.exp2(peak - top)
            result = ((partial[place] * keep + result) / (total * keep + more)).astype(out.dtype)
            for h in range(heads):
                column = ((half + core[0]) % 2 * heads + h) * head_dim
                out[first : first + tile, pl.ds(pl.multiple_of(column, head_dim), head_dim)] = (
                    result[h * tile : (h + 1) * tile]
                )


def attend(core, q_mine, q_other, columns, one_three, three_one, two, own, starts):
    rows, head_dim = own.shape[0], own.shape[1] // 2
    heads = columns // head_dim
    scalar = pl.BlockSpec(memory_space=pltpu.SMEM)
    vector = pl.BlockSpec(memory_space=pltpu.VMEM)
    args = (core, q_mine, q_other, one_three, three_one, own, starts)
    partial, stats = pl.pallas_call(
        functools.partial(near_kernel, heads=heads),
        in_specs=[scalar] + [vector] * (len(args) - 1),
        out_specs=[vector, vector],
        scratch_shapes=[pltpu.VMEM(own.shape, own.dtype)] * 2,
        out_shape=[jax.ShapeDtypeStruct((2 * heads * rows, head_dim), jnp.float32)] * 2,
        compiler_params=pltpu.CompilerParams(vmem_limit_bytes=vmem_bytes),
        cost_estimate=pl.CostEstimate(
            flops=8 * rows * 9 * tile * columns,
            bytes_accessed=16 * rows * columns,
            transcendentals=4 * rows * 9 * tile,
        ),
        name="attend_near",
    )(*args)
    args = (core, q_mine, q_other, two, starts, partial, stats)
    return pl.pallas_call(
        functools.partial(last_kernel, heads=heads),
        in_specs=[scalar] + [vector] * (len(args) - 1),
        out_specs=vector,
        out_shape=jax.ShapeDtypeStruct((rows, 2 * columns), jnp.bfloat16),
        compiler_params=pltpu.CompilerParams(vmem_limit_bytes=vmem_bytes),
        cost_estimate=pl.CostEstimate(
            flops=8 * rows * 4 * tile * columns,
            bytes_accessed=16 * rows * columns,
            transcendentals=4 * rows * 4 * tile,
        ),
        name="attend_last",
    )(*args)


def per_device(tokens, lengths, q_weight, kv_weight):
    rows, features = tokens.shape
    head_dim = kv_weight.shape[2] // 2
    core = lax.axis_index("dp")
    plane = lax.axis_index("z")
    shard = plane * yh_size + lax.axis_index("yh")

    depth = q_weight.shape[0]
    half_cols = q_weight.shape[2] // 2
    columns = half_cols + head_dim
    q_half = lax.dynamic_slice_in_dim(q_weight[:, 0], core * half_cols, half_cols, 1)
    kv_half = lax.dynamic_slice_in_dim(kv_weight[:, 0], core * head_dim, head_dim, 1)
    mine = jnp.concatenate([q_half, kv_half], axis=1)
    block = spread(mine, "yh", yh_size)

    positions = shard * rows + jnp.arange(rows, dtype=jnp.int32)
    half = head_dim // 2
    freqs = jnp.exp(
        jnp.arange(half, dtype=jnp.float32) * (-2.0 * math.log(500000.0) / head_dim)
    )
    angle = positions.astype(jnp.float32)[:, None] * freqs[None, :]
    cosine = jnp.concatenate([jnp.cos(angle)] * 2, axis=1)
    sine = jnp.sin(angle)
    sine = jnp.concatenate([-sine, sine], axis=1)
    docs = jnp.arange(lengths.shape[0])
    ends = jnp.sum(jnp.where(docs[None, :] <= docs[:, None], lengths[None, :], 0), axis=1)
    starts = jnp.max(jnp.where(ends[None, :] <= positions[:, None], ends[None, :], 0), axis=1)
    starts = (starts - (shard - 3) * rows)[:, None]

    block, cosine, sine, starts, tokens = lax.optimization_barrier(
        (block, cosine, sine, starts, tokens)
    )
    tokens_other = swap_cores(tokens)
    ahead, back = ring_pairs(lambda dp: 1 - 2 * dp), ring_pairs(lambda dp: 2 * dp - 1)
    send_ahead = lambda value: lax.ppermute(value, axes, ahead)
    send_back = lambda value: lax.ppermute(value, axes, back)
    steps = jnp.array([0, -1, 1, -2, 2, -3, 3, 4], jnp.int32)
    order = (plane + steps * (1 - 2 * core)) % z_size
    ahead1, back1 = send_ahead(block), send_back(block)
    ahead2, back2 = send_ahead(ahead1), send_back(back1)
    blocks = [block, ahead1, back1]
    (total,) = project_part(order, blocks, [(tokens, [0, 1, 2], None)], "first")
    ahead2, total = lax.optimization_barrier((ahead2, total))
    ahead3, back3 = send_ahead(ahead2), send_back(back2)
    far = lax.ppermute(ahead2, axes, ring_pairs(lambda dp: 2 - 4 * dp))
    blocks += [ahead2, back2]
    totals = project_part(
        order, blocks, [(tokens, [3, 4], total), (tokens_other, [0, 1, 2, 3, 4], None)], "second"
    )
    totals = project_part(
        order[5:7],
        [ahead3, back3],
        [(tokens, [0, 1], totals[0]), (tokens_other, [0, 1], totals[1])],
        "third",
    )
    scalars = jnp.stack([order[7], core])
    mine, theirs = finish(scalars, tokens, tokens_other, far, totals, cosine, sine)
    other = swap_cores(theirs)
    first = core == 0
    kv_mine, kv_other = mine[:, half_cols:], other[:, half_cols:]
    own = jnp.concatenate(
        [lax.select(first, kv_mine, kv_other), lax.select(first, kv_other, kv_mine)], axis=1
    )
    one_three = lax.ppermute(own, axes, shift_pairs(lambda dp: 1 + 2 * dp))
    three_one = lax.ppermute(own, axes, shift_pairs(lambda dp: 3 - 2 * dp))
    two = lax.ppermute(one_three, axes, shift_pairs(lambda dp: 1 - 2 * dp))
    core_index = core.reshape(1).astype(jnp.int32)
    out = attend(core_index, mine, other, half_cols, one_three, three_one, two, own, starts)
    return out[:, None]


def solution(mesh):
    split = Mesh(mesh.devices.reshape(2, z_size, yh_size, x_size, yl_size), axes)
    column = P(("z", "yh"), ("x", "yl"), None)
    return jax.shard_map(
        per_device,
        mesh=split,
        in_specs=(P(("dp", "z", "yh"), None), P("dp"), column, column),
        out_specs=P(("dp", "z", "yh"), ("x", "yl"), None),
        check_vma=False,
    )
```
